256 devices in a mesh: wide: 16 (over x, y), narrow: 16 (over z, core).
Axes of the slice: x: 4, y: 4, z: 8, core: 2. Of those that a mesh axis runs over, the one named last changes fastest.
Arguments:
- model: float32 [512, 2, 256, 256], P(('wide', 'narrow')), may hold values from -6 to 6
- observed: float32 [512, 2, 256, 256], P(('wide', 'narrow')), may hold values from -6 to 6
- own_weights: float32 [5, 512, 2, 256, 256], P(None, ('wide', 'narrow')), may hold values from -0.1875 to 0.1875
- partner_weights: float32 [5, 512, 2, 256, 256], P(None, ('wide', 'narrow')), may hold values from -0.1875 to 0.1875
Outputs:
- residual: float32 [512, 2, 256, 256], P(('wide', 'narrow'))
- gradient: float32 [512, 2, 256, 256], P(('wide', 'narrow'))
The draws below stay inside these ranges and needn't reach their ends.
All inputs are finite; a program needn't handle non-finite values.
Results may differ from the reference program's by a relative error of at most 0.0001.
Values sent between devices are 32-bit elements; how exact they have to be, the bound alone decides.
A program may use at most 128 MiB of HBM per device.

```python
import jax
import jax.numpy as jnp
from jax import lax

K = 256
LEVELS = 5
ROWS = 256
BOXES = 512
N_WIDE = 16
N_NARROW = 16


def level_of(own_key, extent, pieces, smallest, high):
    level, own = 1.0, jax.random.fold_in(own_key, 6)
    for position, parts in pieces:
        heights = jnp.exp(jax.random.uniform(jax.random.fold_in(own, position), (parts,), jnp.float32, smallest / len(pieces), high / len(pieces)))
        level = level * jnp.repeat(heights, extent[position] // parts).reshape([-1 if axis == position else 1 for axis in range(len(extent))])
    return level


def normal_values(own_key, extent, scale, reach, pieces=(), kind=jnp.bfloat16):
    level = level_of(own_key, extent, pieces, -0.22, 0.18) if pieces else 1.0
    array = jax.random.normal(own_key, extent, jnp.float32) * scale * level
    return jnp.minimum(jnp.maximum(array, -reach), reach).astype(kind)


def setup_inputs(seed: int = 0) -> dict:
    key_of = jax.random.split(jax.random.key(seed), 5)
    return {
        "model": normal_values(key_of[0], (BOXES, 2, ROWS, K), 1.0, 6.0, ((0, 256),), jnp.float32),
        "observed": normal_values(key_of[1], (BOXES, 2, ROWS, K), 1.0, 6.0, ((0, 256),), jnp.float32),
        "own_weights": normal_values(key_of[2], (LEVELS, BOXES, 2, K, K), (4 * K) ** -0.5, 0.1875, ((1, 256),), jnp.float32),
        "partner_weights": normal_values(key_of[3], (LEVELS, BOXES, 2, K, K), (4 * K) ** -0.5, 0.1875, ((1, 256),), jnp.float32),
    }


def mult(u, m):
    def prod(a, b):
        return jnp.einsum('brk,bkm->brm', a, b, precision=lax.Precision.HIGHEST)
    ur, ui = u[:, 0], u[:, 1]
    mr, mi = m[:, 0], m[:, 1]
    return jnp.stack([prod(ur, mr) - prod(ui, mi), prod(ur, mi) + prod(ui, mr)], axis=1)


def mult_adjoint(u, m):
    def prod(a, b):
        return jnp.einsum('brm,bkm->brk', a, b, precision=lax.Precision.HIGHEST)
    ur, ui = u[:, 0], u[:, 1]
    mr, mi = m[:, 0], m[:, 1]
    return jnp.stack([prod(ur, mr) + prod(ui, mi), prod(ui, mr) - prod(ur, mi)], axis=1)


def reference(model, observed, own_weights, partner_weights):
    narrow_bits = N_NARROW.bit_length() - 1
    wide_bits = N_WIDE.bit_length() - 1
    shifts = [0, 1, narrow_bits, 1 + narrow_bits, narrow_bits + wide_bits]
    boxes_index = jnp.arange(model.shape[0], dtype=jnp.int32)
    state = model
    for level in range(LEVELS):
        partner = boxes_index ^ (1 << shifts[level])
        state = mult(state, own_weights[level]) + mult(state[partner], partner_weights[level])
    residual = state - observed
    grad = residual
    for level in reversed(range(LEVELS)):
        partner = boxes_index ^ (1 << shifts[level])
        grad = mult_adjoint(grad, own_weights[level]) + mult_adjoint(grad, partner_weights[level])[partner]
    return residual, grad
```

```python
import functools

import jax
import jax.numpy as jnp
from jax import lax
from jax.experimental import pallas as pl
from jax.experimental.pallas import tpu as pltpu
from jax.sharding import PartitionSpec as P

MESH = pl.DeviceIdType.MESH
LEVELS = 5
CHUNKS = 8
DELAYS = (0, 1, 3, 4, 5, 6, 7, 10, 11)
BF16, F32 = jnp.bfloat16, jnp.float32


def split(x):
    high = x.astype(BF16)
    return high, (x - high.astype(F32)).astype(BF16)


def high_low(x):
    high, low = split(x)
    return jnp.concatenate([high, low], axis=0)


def dot(a, b):
    return jnp.dot(a, b, preferred_element_type=F32)


def dot_t(a, b):
    return lax.dot_general(a, b, (((1,), (1,)), ((), ())), preferred_element_type=F32)


def kernel(
    model, observed, own, partner, residual, gradient,
    start, data, own_f32, partner_f32, w_high, w_low,
    state, other, kept, term, carried, res_out, grad_out,
    in_sem, weight_sem, out_sem, send_sem, recv_sem,
):
    rows = model.shape[2]
    k = model.shape[3]
    chunks = state.shape[1]
    size = rows // chunks
    narrow, wide = lax.axis_index("narrow"), lax.axis_index("wide")
    narrow_top, wide_top = lax.axis_size("narrow") // 2, lax.axis_size("wide") // 2
    partners = {
        1: (wide, jnp.bitwise_xor(narrow, 1)),
        2: (wide, jnp.bitwise_xor(narrow, narrow_top)),
        3: (jnp.bitwise_xor(wide, 1), narrow),
        4: (jnp.bitwise_xor(wide, wide_top), narrow),
    }

    copy_in = [
        pltpu.make_async_copy(model, start, in_sem.at[0]),
        pltpu.make_async_copy(observed, data, in_sem.at[1]),
    ]

    def weights_in(level):
        return (
            pltpu.make_async_copy(own.at[level], own_f32.at[level], weight_sem.at[0, level]),
            pltpu.make_async_copy(partner.at[level], partner_f32.at[level], weight_sem.at[1, level]),
        )

    def exchange(level, c, back):
        slot = level - 1
        way = 4 * back + slot
        return pltpu.make_async_remote_copy(
            src_ref=(term if back else state).at[slot, c],
            dst_ref=(carried if back else other).at[slot, c],
            send_sem=send_sem.at[way, c],
            recv_sem=recv_sem.at[way, c],
            device_id=partners[level],
            device_id_type=MESH,
        )

    def copy_out(c, which):
        src, dst = ((res_out, residual), (grad_out, gradient))[which]
        return pltpu.make_async_copy(
            src.at[c], dst.at[:, :, pl.ds(c * size, size), :], out_sem.at[which, c]
        )

    copy_in[0].start()
    for level in range(LEVELS):
        for copy in weights_in(level):
            copy.start()
        if level == 1:
            copy_in[1].start()

    barrier = pltpu.get_barrier_semaphore()
    for level in range(1, LEVELS):
        pl.semaphore_signal(barrier, inc=1, device_id=partners[level], device_id_type=MESH)
    pl.semaphore_wait(barrier, LEVELS - 1)

    def prepare(level):
        for copy in weights_in(level):
            copy.wait()

        @pl.loop(0, 2)
        def _(b):
            for i, source in enumerate((own_f32, partner_f32)):
                for part in range(2):
                    high, low = split(source[level, b, part])
                    place = pl.ds((2 * i + part) * k, k)
                    w_high[level, b, place, :] = high
                    w_low[level, b, place, :] = low

    def forward(level, mine, theirs, b):
        (ur, ui), (vr, vi) = mine, theirs
        real = jnp.concatenate([ur, -ui, vr, -vi], axis=1)
        imag = jnp.concatenate([ui, ur, vi, vr], axis=1)
        high, low = split(jnp.concatenate([real, imag], axis=0))
        both = dot(jnp.concatenate([high, low], axis=0), w_high[level, b])
        out = both[: 2 * size] + both[2 * size :] + dot(high, w_low[level, b])
        return out[:size], out[size:]

    def adjoint_side(gr, gi):
        first = jnp.concatenate([gr, gi], axis=0)
        second = jnp.concatenate([gi, -gr], axis=0)
        return split(jnp.concatenate([first, second], axis=1))

    def adjoint(level, which, side, b):
        high, low = side

        def weight(w):
            return jnp.concatenate(
                [w[level, b, pl.ds((2 * which + part) * k, k), :] for part in range(2)], axis=1
            )

        both = dot_t(jnp.concatenate([high, low], axis=0), weight(w_high))
        out = both[: 2 * size] + both[2 * size :] + dot_t(high, weight(w_low))
        return out[:size], out[size:]

    def put(ref, index, value):
        for part in range(2):
            ref[(*index, part)] = value[part]

    def back_level(level, c, grads):
        sides = [adjoint_side(*g) for g in grads]
        for b in range(2):
            put(term, (level - 1, c, b), adjoint(level, 1, sides[b], b))
        exchange(level, c, 1).start()
        for b in range(2):
            put(kept, (level - 1, c, b), adjoint(level, 0, sides[b], b))

    def arrived(level, c):
        exchange(level, c, 1).wait_recv()
        return [
            [kept[level - 1, c, b, part] + carried[level - 1, c, b, part] for part in range(2)]
            for b in range(2)
        ]

    def first(c):
        @pl.when(c == 0)
        def _():
            copy_in[0].wait()
            prepare(0)

        at = pl.ds(pl.multiple_of(c * size, size), size)
        boxes = [[start[b, part, at, :] for part in range(2)] for b in range(2)]
        for b in range(2):
            put(state, (0, c, b), forward(0, boxes[b], boxes[1 - b], b))
        exchange(1, c, 0).start()

    def middle(level, c):
        @pl.when(c == 0)
        def _():
            prepare(level)

        exchange(level, c, 0).wait_recv()
        slot = level - 1
        for b in range(2):
            mine, theirs = ([ref[slot, c, b, part] for part in range(2)] for ref in (state, other))
            put(state, (slot + 1, c, b), forward(level, mine, theirs, b))
        exchange(level + 1, c, 0).start()

    def turn(c):
        @pl.when(c == 0)
        def _():
            prepare(4)
            copy_in[1].wait()

        exchange(4, c, 0).wait_recv()
        at = pl.ds(pl.multiple_of(c * size, size), size)
        grads = []
        for b in range(2):
            mine, theirs = ([ref[3, c, b, part] for part in range(2)] for ref in (state, other))
            out = forward(4, mine, theirs, b)
            grads.append([out[part] - data[b, part, at, :] for part in range(2)])
            put(res_out, (c, b), grads[b])
        back_level(4, c, grads)
        copy_out(c, 0).start()

    def last(c):
        sides = [adjoint_side(*g) for g in arrived(1, c)]
        for b in range(2):
            mine = adjoint(0, 0, sides[b], b)
            theirs = adjoint(0, 1, sides[1 - b], 1 - b)
            put(grad_out, (c, b), [mine[part] + theirs[part] for part in range(2)])
        copy_out(c, 1).start()

    tasks = [
        first,
        functools.partial(middle, 1),
        functools.partial(middle, 2),
        functools.partial(middle, 3),
        turn,
        lambda c: back_level(3, c, arrived(4, c)),
        lambda c: back_level(2, c, arrived(3, c)),
        lambda c: back_level(1, c, arrived(2, c)),
        last,
    ]

    @pl.loop(0, chunks + DELAYS[-1])
    def _(step):
        for task, delay in zip(tasks, DELAYS):
            c = step - delay
            pl.when(jnp.logical_and(c >= 0, c < chunks))(functools.partial(task, c))

    @pl.loop(0, chunks)
    def _(c):
        for back in range(2):
            for level in range(1, LEVELS):
                exchange(level, c, back).wait_send()
        for which in range(2):
            copy_out(c, which).wait()


def shards(model, observed, own, partner):
    boxes, parts, rows, k = model.shape
    size = rows // CHUNKS
    chunked = (CHUNKS, boxes, parts, size, k)
    whole = pltpu.VMEM((LEVELS - 1, *chunked), F32)
    flops = 2 * 2 * LEVELS * boxes * 8 * rows * k * k * 3
    return pl.pallas_call(
        kernel,
        out_shape=[jax.ShapeDtypeStruct(model.shape, F32)] * 2,
        in_specs=[pl.BlockSpec(memory_space=pltpu.HBM)] * 4,
        out_specs=[pl.BlockSpec(memory_space=pltpu.HBM)] * 2,
        scratch_shapes=[
            pltpu.VMEM(model.shape, F32),
            pltpu.VMEM(model.shape, F32),
            pltpu.VMEM(own.shape, F32),
            pltpu.VMEM(own.shape, F32),
            pltpu.VMEM((LEVELS, boxes, 4 * k, k), BF16),
            pltpu.VMEM((LEVELS, boxes, 4 * k, k), BF16),
            whole, whole, whole, whole, whole,
            pltpu.VMEM(chunked, F32),
            pltpu.VMEM(chunked, F32),
            pltpu.SemaphoreType.DMA((2,)),
            pltpu.SemaphoreType.DMA((2, LEVELS)),
            pltpu.SemaphoreType.DMA((2, CHUNKS)),
            pltpu.SemaphoreType.DMA((8, CHUNKS)),
            pltpu.SemaphoreType.DMA((8, CHUNKS)),
        ],
        compiler_params=pltpu.CompilerParams(
            collective_id=0, has_side_effects=True, vmem_limit_bytes=58 * 2**20
        ),
        cost_estimate=pl.CostEstimate(flops=flops, bytes_accessed=14 * 2**20, transcendentals=0),
    )(model, observed, own, partner)


def solution(mesh):
    boxes = P(("wide", "narrow"), None, None, None)
    weights = P(None, ("wide", "narrow"), None, None, None)
    return jax.shard_map(
        shards,
        mesh=mesh,
        in_specs=(boxes, boxes, weights, weights),
        out_specs=(boxes, boxes),
        check_vma=False,
    )
```

```python
import functools

import jax
import jax.numpy as jnp
from jax import lax
from jax.experimental import pallas as pl
from jax.experimental.pallas import tpu as pltpu
from jax.sharding import PartitionSpec as P

MESH = pl.DeviceIdType.MESH
LEVELS = 5
CHUNKS = 8
DELAYS = (0, 1, 3, 4, 5, 6, 7, 10, 11)
BF16, F32 = jnp.bfloat16, jnp.float32


def split(x):
    high = x.astype(BF16)
    return high, (x - high.astype(F32)).astype(BF16)


def high_low(x):
    high, low = split(x)
    return jnp.concatenate([high, low], axis=0)


def dot(a, b):
    return jnp.dot(a, b, preferred_element_type=F32)


def dot_t(a, b):
    return lax.dot_general(a, b, (((1,), (1,)), ((), ())), preferred_element_type=F32)


def kernel(
    model, observed, own, partner, residual, gradient,
    start, data, own_f32, partner_f32, w_high, w_low,
    state, other, kept, term, carried,
    in_sem, weight_sem, send_sem, recv_sem,
):
    rows = model.shape[2]
    k = model.shape[3]
    chunks = state.shape[1]
    size = rows // chunks
    narrow, wide = lax.axis_index("narrow"), lax.axis_index("wide")
    narrow_top, wide_top = lax.axis_size("narrow") // 2, lax.axis_size("wide") // 2
    partners = {
        1: (wide, jnp.bitwise_xor(narrow, 1)),
        2: (wide, jnp.bitwise_xor(narrow, narrow_top)),
        3: (jnp.bitwise_xor(wide, 1), narrow),
        4: (jnp.bitwise_xor(wide, wide_top), narrow),
    }

    copy_in = [
        pltpu.make_async_copy(model, start, in_sem.at[0]),
        pltpu.make_async_copy(observed, data, in_sem.at[1]),
    ]

    def weights_in(level):
        return (
            pltpu.make_async_copy(own.at[level], own_f32.at[level], weight_sem.at[0, level]),
            pltpu.make_async_copy(partner.at[level], partner_f32.at[level], weight_sem.at[1, level]),
        )

    def exchange(level, c, back):
        slot = level - 1
        way = 4 * back + slot
        return pltpu.make_async_remote_copy(
            src_ref=(term if back else state).at[slot, c],
            dst_ref=(carried if back else other).at[slot, c],
            send_sem=send_sem.at[way, c],
            recv_sem=recv_sem.at[way, c],
            device_id=partners[level],
            device_id_type=MESH,
        )

    copy_in[0].start()
    for copy in weights_in(0):
        copy.start()

    barrier = pltpu.get_barrier_semaphore()
    for level in range(1, LEVELS):
        pl.semaphore_signal(barrier, inc=1, device_id=partners[level], device_id_type=MESH)

    def prepare(level):
        for copy in weights_in(level):
            copy.wait()

        @pl.loop(0, 2)
        def _(b):
            for i, source in enumerate((own_f32, partner_f32)):
                for part in range(2):
                    high, low = split(source[level, b, part])
                    place = pl.ds((2 * i + part) * k, k)
                    w_high[level, b, place, :] = high
                    w_low[level, b, place, :] = low

    def forward(level, mine, theirs, b):
        (ur, ui), (vr, vi) = mine, theirs
        real = jnp.concatenate([ur, -ui, vr, -vi], axis=1)
        imag = jnp.concatenate([ui, ur, vi, vr], axis=1)
        high, low = split(jnp.concatenate([real, imag], axis=0))
        both = dot(jnp.concatenate([high, low], axis=0), w_high[level, b])
        out = both[: 2 * size] + both[2 * size :] + dot(high, w_low[level, b])
        return out[:size], out[size:]

    def adjoint_side(gr, gi):
        first = jnp.concatenate([gr, gi], axis=0)
        second = jnp.concatenate([gi, -gr], axis=0)
        return split(jnp.concatenate([first, second], axis=1))

    def adjoint(level, which, side, b):
        high, low = side

        def weight(w):
            return jnp.concatenate(
                [w[level, b, pl.ds((2 * which + part) * k, k), :] for part in range(2)], axis=1
            )

        both = dot_t(jnp.concatenate([high, low], axis=0), weight(w_high))
        out = both[: 2 * size] + both[2 * size :] + dot_t(high, weight(w_low))
        return out[:size], out[size:]

    def put(ref, index, value):
        for part in range(2):
            ref[(*index, part)] = value[part]

    def back_level(level, c, grads):
        sides = [adjoint_side(*g) for g in grads]
        for b in range(2):
            put(term, (level - 1, c, b), adjoint(level, 1, sides[b], b))
        exchange(level, c, 1).start()
        for b in range(2):
            put(kept, (level - 1, c, b), adjoint(level, 0, sides[b], b))

    def arrived(level, c):
        exchange(level, c, 1).wait_recv()
        return [
            [kept[level - 1, c, b, part] + carried[level - 1, c, b, part] for part in range(2)]
            for b in range(2)
        ]

    def first(c):
        at = pl.ds(pl.multiple_of(c * size, size), size)
        boxes = [[start[b, part, at, :] for part in range(2)] for b in range(2)]
        for b in range(2):
            put(state, (0, c, b), forward(0, boxes[b], boxes[1 - b], b))

        @pl.when(c == 0)
        def _():
            pl.semaphore_wait(barrier, LEVELS - 1)

        exchange(1, c, 0).start()

    def middle(level, c):
        @pl.when(c == 0)
        def _():
            prepare(level)

        exchange(level, c, 0).wait_recv()
        slot = level - 1
        for b in range(2):
            mine, theirs = ([ref[slot, c, b, part] for part in range(2)] for ref in (state, other))
            put(state, (slot + 1, c, b), forward(level, mine, theirs, b))
        exchange(level + 1, c, 0).start()

    def turn(c):
        @pl.when(c == 0)
        def _():
            prepare(4)
            copy_in[1].wait()

        exchange(4, c, 0).wait_recv()
        at = pl.ds(pl.multiple_of(c * size, size), size)
        grads = []
        for b in range(2):
            mine, theirs = ([ref[3, c, b, part] for part in range(2)] for ref in (state, other))
            out = forward(4, mine, theirs, b)
            grads.append([out[part] - data[b, part, at, :] for part in range(2)])
            for part in range(2):
                residual[b, part, at, :] = grads[b][part]
        back_level(4, c, grads)

    def last(c):
        sides = [adjoint_side(*g) for g in arrived(1, c)]
        at = pl.ds(pl.multiple_of(c * size, size), size)
        for b in range(2):
            mine = adjoint(0, 0, sides[b], b)
            theirs = adjoint(0, 1, sides[1 - b], 1 - b)
            for part in range(2):
                gradient[b, part, at, :] = mine[part] + theirs[part]

    tasks = [
        first,
        functools.partial(middle, 1),
        functools.partial(middle, 2),
        functools.partial(middle, 3),
        turn,
        lambda c: back_level(3, c, arrived(4, c)),
        lambda c: back_level(2, c, arrived(3, c)),
        lambda c: back_level(1, c, arrived(2, c)),
        last,
    ]

    copy_in[0].wait()
    prepare(0)
    for level in range(1, LEVELS):
        for copy in weights_in(level):
            copy.start()
    copy_in[1].start()

    @pl.loop(0, chunks + DELAYS[-1])
    def _(step):
        for task, delay in zip(tasks, DELAYS):
            c = step - delay
            pl.when(jnp.logical_and(c >= 0, c < chunks))(functools.partial(task, c))

    @pl.loop(0, chunks)
    def _(c):
        for back in range(2):
            for level in range(1, LEVELS):
                exchange(level, c, back).wait_send()


def shards(model, observed, own, partner):
    boxes, parts, rows, k = model.shape
    size = rows // CHUNKS
    chunked = (CHUNKS, boxes, parts, size, k)
    whole = pltpu.VMEM((LEVELS - 1, *chunked), F32)
    flops = 2 * 2 * LEVELS * boxes * 8 * rows * k * k * 3
    return pl.pallas_call(
        kernel,
        out_shape=[jax.ShapeDtypeStruct(model.shape, F32)] * 2,
        in_specs=[pl.BlockSpec(memory_space=pltpu.HBM)] * 4,
        out_specs=[pl.BlockSpec(memory_space=pltpu.VMEM)] * 2,
        scratch_shapes=[
            pltpu.VMEM(model.shape, F32),
            pltpu.VMEM(model.shape, F32),
            pltpu.VMEM(own.shape, F32),
            pltpu.VMEM(own.shape, F32),
            pltpu.VMEM((LEVELS, boxes, 4 * k, k), BF16),
            pltpu.VMEM((LEVELS, boxes, 4 * k, k), BF16),
            whole, whole, whole, whole, whole,
            pltpu.SemaphoreType.DMA((2,)),
            pltpu.SemaphoreType.DMA((2, LEVELS)),
            pltpu.SemaphoreType.DMA((8, CHUNKS)),
            pltpu.SemaphoreType.DMA((8, CHUNKS)),
        ],
        compiler_params=pltpu.CompilerParams(
            collective_id=0, has_side_effects=True, vmem_limit_bytes=51 * 2**20
        ),
        cost_estimate=pl.CostEstimate(flops=flops, bytes_accessed=14 * 2**20, transcendentals=0),
    )(model, observed, own, partner)


def solution(mesh):
    boxes = P(("wide", "narrow"), None, None, None)
    weights = P(None, ("wide", "narrow"), None, None, None)
    return jax.shard_map(
        shards,
        mesh=mesh,
        in_specs=(boxes, boxes, weights, weights),
        out_specs=(boxes, boxes),
        check_vma=False,
    )
```

```python
import functools

import jax
import jax.numpy as jnp
from jax import lax
from jax.experimental import pallas as pl
from jax.experimental.pallas import tpu as pltpu
from jax.sharding import PartitionSpec as P

MESH = pl.DeviceIdType.MESH
LEVELS = 5
CHUNKS = 8
DELAYS = (0, 1, 3, 4, 5, 6, 7, 10, 11)
AHEAD = 3
BF16, F32 = jnp.bfloat16, jnp.float32


def split(x):
    high = x.astype(BF16)
    return high, (x - high.astype(F32)).astype(BF16)


def high_low(x):
    high, low = split(x)
    return jnp.concatenate([high, low], axis=0)


def dot(a, b):
    return jnp.dot(a, b, preferred_element_type=F32)


def dot_t(a, b):
    return lax.dot_general(a, b, (((1,), (1,)), ((), ())), preferred_element_type=F32)


def kernel(
    model, observed, own, partner, residual, gradient,
    start, data, own_f32, partner_f32, w_high, w_low,
    state, other, kept, term, carried,
    in_sem, weight_sem, send_sem, recv_sem, pace_sem,
):
    rows = model.shape[2]
    k = model.shape[3]
    chunks = state.shape[1]
    size = rows // chunks
    narrow, wide = lax.axis_index("narrow"), lax.axis_index("wide")
    narrow_top, wide_top = lax.axis_size("narrow") // 2, lax.axis_size("wide") // 2
    partners = {
        1: (wide, jnp.bitwise_xor(narrow, 1)),
        2: (wide, jnp.bitwise_xor(narrow, narrow_top)),
        3: (jnp.bitwise_xor(wide, 1), narrow),
        4: (jnp.bitwise_xor(wide, wide_top), narrow),
    }

    neighbour = (wide, jnp.bitwise_xor(narrow, 2))

    copy_in = [
        pltpu.make_async_copy(model, start, in_sem.at[0]),
        pltpu.make_async_copy(observed, data, in_sem.at[1]),
    ]

    def weights_in(level):
        return (
            pltpu.make_async_copy(own.at[level], own_f32.at[level], weight_sem.at[0, level]),
            pltpu.make_async_copy(partner.at[level], partner_f32.at[level], weight_sem.at[1, level]),
        )

    def exchange(level, c, back):
        slot = level - 1
        way = 4 * back + slot
        return pltpu.make_async_remote_copy(
            src_ref=(term if back else state).at[slot, c],
            dst_ref=(carried if back else other).at[slot, c],
            send_sem=send_sem.at[way, c],
            recv_sem=recv_sem.at[way, c],
            device_id=partners[level],
            device_id_type=MESH,
        )

    copy_in[0].start()
    for copy in weights_in(0):
        copy.start()

    barrier = pltpu.get_barrier_semaphore()
    for level in range(1, LEVELS):
        pl.semaphore_signal(barrier, inc=1, device_id=partners[level], device_id_type=MESH)
    pl.semaphore_signal(barrier, inc=1, device_id=neighbour, device_id_type=MESH)

    def prepare(level):
        for copy in weights_in(level):
            copy.wait()

        @pl.loop(0, 2)
        def _(b):
            for i, source in enumerate((own_f32, partner_f32)):
                for part in range(2):
                    high, low = split(source[level, b, part])
                    place = pl.ds((2 * i + part) * k, k)
                    w_high[level, b, place, :] = high
                    w_low[level, b, place, :] = low

    def forward(level, mine, theirs, b):
        (ur, ui), (vr, vi) = mine, theirs
        real = jnp.concatenate([ur, -ui, vr, -vi], axis=1)
        imag = jnp.concatenate([ui, ur, vi, vr], axis=1)
        high, low = split(jnp.concatenate([real, imag], axis=0))
        both = dot(jnp.concatenate([high, low], axis=0), w_high[level, b])
        out = both[: 2 * size] + both[2 * size :] + dot(high, w_low[level, b])
        return out[:size], out[size:]

    def adjoint_side(gr, gi):
        first = jnp.concatenate([gr, gi], axis=0)
        second = jnp.concatenate([gi, -gr], axis=0)
        return split(jnp.concatenate([first, second], axis=1))

    def adjoint(level, which, side, b):
        high, low = side

        def weight(w):
            return jnp.concatenate(
                [w[level, b, pl.ds((2 * which + part) * k, k), :] for part in range(2)], axis=1
            )

        both = dot_t(jnp.concatenate([high, low], axis=0), weight(w_high))
        out = both[: 2 * size] + both[2 * size :] + dot_t(high, weight(w_low))
        return out[:size], out[size:]

    def put(ref, index, value):
        for part in range(2):
            ref[(*index, part)] = value[part]

    def back_level(level, c, grads):
        sides = [adjoint_side(*g) for g in grads]
        for b in range(2):
            put(term, (level - 1, c, b), adjoint(level, 1, sides[b], b))
        exchange(level, c, 1).start()
        for b in range(2):
            put(kept, (level - 1, c, b), adjoint(level, 0, sides[b], b))

    def arrived(level, c):
        exchange(level, c, 1).wait_recv()
        return [
            [kept[level - 1, c, b, part] + carried[level - 1, c, b, part] for part in range(2)]
            for b in range(2)
        ]

    def first(c):
        at = pl.ds(pl.multiple_of(c * size, size), size)
        boxes = [[start[b, part, at, :] for part in range(2)] for b in range(2)]
        for b in range(2):
            put(state, (0, c, b), forward(0, boxes[b], boxes[1 - b], b))

        @pl.when(c == 0)
        def _():
            pl.semaphore_wait(barrier, LEVELS)

        exchange(1, c, 0).start()

    def middle(level, c):
        @pl.when(c == 0)
        def _():
            prepare(level)

        exchange(level, c, 0).wait_recv()
        if level == 2:
            pl.semaphore_signal(pace_sem, inc=1, device_id=neighbour, device_id_type=MESH)
        slot = level - 1
        for b in range(2):
            mine, theirs = ([ref[slot, c, b, part] for part in range(2)] for ref in (state, other))
            put(state, (slot + 1, c, b), forward(level, mine, theirs, b))
        if level == 1:
            @pl.when(c >= AHEAD)
            def _():
                pl.semaphore_wait(pace_sem, 1)

        exchange(level + 1, c, 0).start()

    def turn(c):
        @pl.when(c == 0)
        def _():
            prepare(4)
            copy_in[1].wait()

        exchange(4, c, 0).wait_recv()
        at = pl.ds(pl.multiple_of(c * size, size), size)
        grads = []
        for b in range(2):
            mine, theirs = ([ref[3, c, b, part] for part in range(2)] for ref in (state, other))
            out = forward(4, mine, theirs, b)
            grads.append([out[part] - data[b, part, at, :] for part in range(2)])
            for part in range(2):
                residual[b, part, at, :] = grads[b][part]
        back_level(4, c, grads)

    def last(c):
        sides = [adjoint_side(*g) for g in arrived(1, c)]
        at = pl.ds(pl.multiple_of(c * size, size), size)
        for b in range(2):
            mine = adjoint(0, 0, sides[b], b)
            theirs = adjoint(0, 1, sides[1 - b], 1 - b)
            for part in range(2):
                gradient[b, part, at, :] = mine[part] + theirs[part]

    tasks = [
        first,
        functools.partial(middle, 1),
        functools.partial(middle, 2),
        functools.partial(middle, 3),
        turn,
        lambda c: back_level(3, c, arrived(4, c)),
        lambda c: back_level(2, c, arrived(3, c)),
        lambda c: back_level(1, c, arrived(2, c)),
        last,
    ]

    copy_in[0].wait()
    prepare(0)
    for level in range(1, LEVELS):
        for copy in weights_in(level):
            copy.start()
    copy_in[1].start()

    @pl.loop(0, chunks + DELAYS[-1])
    def _(step):
        for task, delay in zip(tasks, DELAYS):
            c = step - delay
            pl.when(jnp.logical_and(c >= 0, c < chunks))(functools.partial(task, c))

    pl.semaphore_wait(pace_sem, min(AHEAD, chunks))

    @pl.loop(0, chunks)
    def _(c):
        for back in range(2):
            for level in range(1, LEVELS):
                exchange(level, c, back).wait_send()


def write_back(residual, gradient, residual_out, gradient_out, sem):
    copies = [
        pltpu.make_async_copy(source, target, sem.at[i])
        for i, (source, target) in enumerate(((residual, residual_out), (gradient, gradient_out)))
    ]
    for copy in copies:
        copy.start()
    for copy in copies:
        copy.wait()


def shards(model, observed, own, partner):
    boxes, parts, rows, k = model.shape
    size = rows // CHUNKS
    chunked = (CHUNKS, boxes, parts, size, k)
    whole = pltpu.VMEM((LEVELS - 1, *chunked), F32)
    flops = 2 * 2 * LEVELS * boxes * 8 * rows * k * k * 3
    results = pl.pallas_call(
        kernel,
        out_shape=[jax.ShapeDtypeStruct(model.shape, F32)] * 2,
        in_specs=[pl.BlockSpec(memory_space=pltpu.HBM)] * 4,
        out_specs=[pl.BlockSpec(memory_space=pltpu.VMEM)] * 2,
        scratch_shapes=[
            pltpu.VMEM(model.shape, F32),
            pltpu.VMEM(model.shape, F32),
            pltpu.VMEM(own.shape, F32),
            pltpu.VMEM(own.shape, F32),
            pltpu.VMEM((LEVELS, boxes, 4 * k, k), BF16),
            pltpu.VMEM((LEVELS, boxes, 4 * k, k), BF16),
            whole, whole, whole, whole, whole,
            pltpu.SemaphoreType.DMA((2,)),
            pltpu.SemaphoreType.DMA((2, LEVELS)),
            pltpu.SemaphoreType.DMA((8, CHUNKS)),
            pltpu.SemaphoreType.DMA((8, CHUNKS)),
            pltpu.SemaphoreType.REGULAR,
        ],
        compiler_params=pltpu.CompilerParams(
            collective_id=0, has_side_effects=True, vmem_limit_bytes=51 * 2**20
        ),
        cost_estimate=pl.CostEstimate(flops=flops, bytes_accessed=14 * 2**20, transcendentals=0),
    )(model, observed, own, partner)
    return pl.pallas_call(
        write_back,
        out_shape=[jax.ShapeDtypeStruct(model.shape, F32)] * 2,
        in_specs=[pl.BlockSpec(memory_space=pl.ANY)] * 2,
        out_specs=[pl.BlockSpec(memory_space=pltpu.HBM)] * 2,
        scratch_shapes=[pltpu.SemaphoreType.DMA((2,))],
        compiler_params=pltpu.CompilerParams(vmem_limit_bytes=2**20),
        cost_estimate=pl.CostEstimate(flops=0, bytes_accessed=4 * 2**20, transcendentals=0),
    )(*results)


def solution(mesh):
    boxes = P(("wide", "narrow"), None, None, None)
    weights = P(None, ("wide", "narrow"), None, None, None)
    return jax.shard_map(
        shards,
        mesh=mesh,
        in_specs=(boxes, boxes, weights, weights),
        out_specs=(boxes, boxes),
        check_vma=False,
    )
```

```python
import functools

import jax
import jax.numpy as jnp
from jax import lax
from jax.experimental import pallas as pl
from jax.experimental.pallas import tpu as pltpu
from jax.sharding import PartitionSpec as P

MESH = pl.DeviceIdType.MESH
LEVELS = 5
CHUNKS = 8
DELAYS = (0, 1, 3, 4, 5, 6, 7, 10, 11)
AHEAD = 3
BF16, F32 = jnp.bfloat16, jnp.float32


def split(x):
    high = x.astype(BF16)
    return high, (x - high.astype(F32)).astype(BF16)


def high_low(x):
    high, low = split(x)
    return jnp.concatenate([high, low], axis=0)


def dot(a, b):
    return jnp.dot(a, b, preferred_element_type=F32)


def dot_t(a, b):
    return lax.dot_general(a, b, (((1,), (1,)), ((), ())), preferred_element_type=F32)


def kernel(
    model, observed, own, partner, residual, gradient,
    start, data, own_f32, partner_f32, w_high, w_low,
    state, other, kept, term, carried,
    in_sem, weight_sem, send_sem, recv_sem, pace_sem,
):
    rows = model.shape[2]
    k = model.shape[3]
    chunks = state.shape[1]
    size = rows // chunks
    narrow, wide = lax.axis_index("narrow"), lax.axis_index("wide")
    narrow_top, wide_top = lax.axis_size("narrow") // 2, lax.axis_size("wide") // 2
    partners = {
        1: (wide, jnp.bitwise_xor(narrow, 1)),
        2: (wide, jnp.bitwise_xor(narrow, narrow_top)),
        3: (jnp.bitwise_xor(wide, 1), narrow),
        4: (jnp.bitwise_xor(wide, wide_top), narrow),
    }

    neighbour = (wide, jnp.bitwise_xor(narrow, 2))

    copy_in = [
        pltpu.make_async_copy(model, start, in_sem.at[0]),
        pltpu.make_async_copy(observed, data, in_sem.at[1]),
    ]

    def weights_in(level, b):
        return [
            pltpu.make_async_copy(source.at[level, b], target.at[level, b], weight_sem.at[i, level, b])
            for i, (source, target) in enumerate(((own, own_f32), (partner, partner_f32)))
        ]

    def exchange(level, c, back):
        slot = level - 1
        way = 4 * back + slot
        return pltpu.make_async_remote_copy(
            src_ref=(term if back else state).at[slot, c],
            dst_ref=(carried if back else other).at[slot, c],
            send_sem=send_sem.at[way, c],
            recv_sem=recv_sem.at[way, c],
            device_id=partners[level],
            device_id_type=MESH,
        )

    for copy in [*weights_in(0, 0), copy_in[0], *weights_in(0, 1)]:
        copy.start()

    barrier = pltpu.get_barrier_semaphore()
    for level in range(1, LEVELS):
        pl.semaphore_signal(barrier, inc=1, device_id=partners[level], device_id_type=MESH)
    pl.semaphore_signal(barrier, inc=1, device_id=neighbour, device_id_type=MESH)

    def prepare(level):
        for b in range(2):
            for copy in weights_in(level, b):
                copy.wait()
            for i, source in enumerate((own_f32, partner_f32)):
                for part in range(2):
                    high, low = split(source[level, b, part])
                    place = pl.ds((2 * i + part) * k, k)
                    w_high[level, b, place, :] = high
                    w_low[level, b, place, :] = low

    def forward(level, mine, theirs, b):
        (ur, ui), (vr, vi) = mine, theirs
        real = jnp.concatenate([ur, -ui, vr, -vi], axis=1)
        imag = jnp.concatenate([ui, ur, vi, vr], axis=1)
        high, low = split(jnp.concatenate([real, imag], axis=0))
        both = dot(jnp.concatenate([high, low], axis=0), w_high[level, b])
        out = both[: 2 * size] + both[2 * size :] + dot(high, w_low[level, b])
        return out[:size], out[size:]

    def adjoint_side(gr, gi):
        first = jnp.concatenate([gr, gi], axis=0)
        second = jnp.concatenate([gi, -gr], axis=0)
        return split(jnp.concatenate([first, second], axis=1))

    def adjoint(level, which, side, b):
        high, low = side

        def weight(w):
            return jnp.concatenate(
                [w[level, b, pl.ds((2 * which + part) * k, k), :] for part in range(2)], axis=1
            )

        both = dot_t(jnp.concatenate([high, low], axis=0), weight(w_high))
        out = both[: 2 * size] + both[2 * size :] + dot_t(high, weight(w_low))
        return out[:size], out[size:]

    def put(ref, index, value):
        for part in range(2):
            ref[(*index, part)] = value[part]

    def back_level(level, c, grads):
        sides = [adjoint_side(*g) for g in grads]
        for b in range(2):
            put(term, (level - 1, c, b), adjoint(level, 1, sides[b], b))
        exchange(level, c, 1).start()
        for b in range(2):
            put(kept, (level - 1, c, b), adjoint(level, 0, sides[b], b))

    def arrived(level, c):
        exchange(level, c, 1).wait_recv()
        return [
            [kept[level - 1, c, b, part] + carried[level - 1, c, b, part] for part in range(2)]
            for b in range(2)
        ]

    def first(c):
        at = pl.ds(pl.multiple_of(c * size, size), size)
        boxes = [[start[b, part, at, :] for part in range(2)] for b in range(2)]
        for b in range(2):
            put(state, (0, c, b), forward(0, boxes[b], boxes[1 - b], b))

        @pl.when(c == 0)
        def _():
            pl.semaphore_wait(barrier, LEVELS)

        exchange(1, c, 0).start()

    def middle(level, c):
        @pl.when(c == 0)
        def _():
            prepare(level)

        exchange(level, c, 0).wait_recv()
        if level == 2:
            pl.semaphore_signal(pace_sem, inc=1, device_id=neighbour, device_id_type=MESH)
        slot = level - 1
        for b in range(2):
            mine, theirs = ([ref[slot, c, b, part] for part in range(2)] for ref in (state, other))
            put(state, (slot + 1, c, b), forward(level, mine, theirs, b))
        if level == 1:
            @pl.when(c >= AHEAD)
            def _():
                pl.semaphore_wait(pace_sem, 1)

        exchange(level + 1, c, 0).start()

    def turn(c):
        @pl.when(c == 0)
        def _():
            prepare(4)
            copy_in[1].wait()

        exchange(4, c, 0).wait_recv()
        at = pl.ds(pl.multiple_of(c * size, size), size)
        grads = []
        for b in range(2):
            mine, theirs = ([ref[3, c, b, part] for part in range(2)] for ref in (state, other))
            out = forward(4, mine, theirs, b)
            grads.append([out[part] - data[b, part, at, :] for part in range(2)])
            for part in range(2):
                residual[b, part, at, :] = grads[b][part]
        back_level(4, c, grads)

    def last(c):
        sides = [adjoint_side(*g) for g in arrived(1, c)]
        at = pl.ds(pl.multiple_of(c * size, size), size)
        for b in range(2):
            mine = adjoint(0, 0, sides[b], b)
            theirs = adjoint(0, 1, sides[1 - b], 1 - b)
            for part in range(2):
                gradient[b, part, at, :] = mine[part] + theirs[part]

    tasks = [
        first,
        functools.partial(middle, 1),
        functools.partial(middle, 2),
        functools.partial(middle, 3),
        turn,
        lambda c: back_level(3, c, arrived(4, c)),
        lambda c: back_level(2, c, arrived(3, c)),
        lambda c: back_level(1, c, arrived(2, c)),
        last,
    ]

    prepare(0)
    copy_in[0].wait()
    for level in range(1, LEVELS):
        for copy in [*weights_in(level, 0), *weights_in(level, 1)]:
            copy.start()
    copy_in[1].start()

    @pl.loop(0, chunks + DELAYS[-1])
    def _(step):
        for task, delay in zip(tasks, DELAYS):
            c = step - delay
            pl.when(jnp.logical_and(c >= 0, c < chunks))(functools.partial(task, c))

    pl.semaphore_wait(pace_sem, min(AHEAD, chunks))

    @pl.loop(0, chunks)
    def _(c):
        for back in range(2):
            for level in range(1, LEVELS):
                exchange(level, c, back).wait_send()


def write_back(residual, gradient, residual_out, gradient_out, sem):
    copies = [
        pltpu.make_async_copy(source, target, sem.at[i])
        for i, (source, target) in enumerate(((residual, residual_out), (gradient, gradient_out)))
    ]
    for copy in copies:
        copy.start()
    for copy in copies:
        copy.wait()


def shards(model, observed, own, partner):
    boxes, parts, rows, k = model.shape
    size = rows // CHUNKS
    chunked = (CHUNKS, boxes, parts, size, k)
    whole = pltpu.VMEM((LEVELS - 1, *chunked), F32)
    flops = 2 * 2 * LEVELS * boxes * 8 * rows * k * k * 3
    results = pl.pallas_call(
        kernel,
        out_shape=[jax.ShapeDtypeStruct(model.shape, F32)] * 2,
        in_specs=[pl.BlockSpec(memory_space=pltpu.HBM)] * 4,
        out_specs=[pl.BlockSpec(memory_space=pltpu.VMEM)] * 2,
        scratch_shapes=[
            pltpu.VMEM(model.shape, F32),
            pltpu.VMEM(model.shape, F32),
            pltpu.VMEM(own.shape, F32),
            pltpu.VMEM(own.shape, F32),
            pltpu.VMEM((LEVELS, boxes, 4 * k, k), BF16),
            pltpu.VMEM((LEVELS, boxes, 4 * k, k), BF16),
            whole, whole, whole, whole, whole,
            pltpu.SemaphoreType.DMA((2,)),
            pltpu.SemaphoreType.DMA((2, LEVELS, 2)),
            pltpu.SemaphoreType.DMA((8, CHUNKS)),
            pltpu.SemaphoreType.DMA((8, CHUNKS)),
            pltpu.SemaphoreType.REGULAR,
        ],
        compiler_params=pltpu.CompilerParams(
            collective_id=0, has_side_effects=True, vmem_limit_bytes=51 * 2**20
        ),
        cost_estimate=pl.CostEstimate(flops=flops, bytes_accessed=14 * 2**20, transcendentals=0),
    )(model, observed, own, partner)
    return pl.pallas_call(
        write_back,
        out_shape=[jax.ShapeDtypeStruct(model.shape, F32)] * 2,
        in_specs=[pl.BlockSpec(memory_space=pl.ANY)] * 2,
        out_specs=[pl.BlockSpec(memory_space=pltpu.HBM)] * 2,
        scratch_shapes=[pltpu.SemaphoreType.DMA((2,))],
        compiler_params=pltpu.CompilerParams(vmem_limit_bytes=2**20),
        cost_estimate=pl.CostEstimate(flops=0, bytes_accessed=4 * 2**20, transcendentals=0),
    )(*results)


def solution(mesh):
    boxes = P(("wide", "narrow"), None, None, None)
    weights = P(None, ("wide", "narrow"), None, None, None)
    return jax.shard_map(
        shards,
        mesh=mesh,
        in_specs=(boxes, boxes, weights, weights),
        out_specs=(boxes, boxes),
        check_vma=False,
    )
```

```python
import functools

import jax
import jax.numpy as jnp
from jax import lax
from jax.experimental import pallas as pl
from jax.experimental.pallas import tpu as pltpu
from jax.sharding import PartitionSpec as P

MESH = pl.DeviceIdType.MESH
LEVELS = 5
CHUNKS = 8
DELAYS = (0, 1, 3, 4, 5, 6, 7, 10, 11)
AHEAD = 3
BF16, F32 = jnp.bfloat16, jnp.float32


def split(x):
    high = x.astype(BF16)
    return high, (x - high.astype(F32)).astype(BF16)


def high_low(x):
    high, low = split(x)
    return jnp.concatenate([high, low], axis=0)


def dot(a, b):
    return jnp.dot(a, b, preferred_element_type=F32)


def dot_t(a, b):
    return lax.dot_general(a, b, (((1,), (1,)), ((), ())), preferred_element_type=F32)


def kernel(
    model, observed, own, partner, residual, gradient,
    start, data, own_f32, partner_f32, w_high, w_low,
    state, other, kept, term, carried,
    in_sem, weight_sem, send_sem, recv_sem, pace_sem,
):
    rows = model.shape[2]
    k = model.shape[3]
    chunks = state.shape[1]
    size = rows // chunks
    narrow, wide = lax.axis_index("narrow"), lax.axis_index("wide")
    narrow_top, wide_top = lax.axis_size("narrow") // 2, lax.axis_size("wide") // 2
    partners = {
        1: (wide, jnp.bitwise_xor(narrow, 1)),
        2: (wide, jnp.bitwise_xor(narrow, narrow_top)),
        3: (jnp.bitwise_xor(wide, 1), narrow),
        4: (jnp.bitwise_xor(wide, wide_top), narrow),
    }

    neighbour = (wide, jnp.bitwise_xor(narrow, 2))

    copy_in = [
        pltpu.make_async_copy(model, start, in_sem.at[0]),
        pltpu.make_async_copy(observed, data, in_sem.at[1]),
    ]

    def weights_in(level):
        return (
            pltpu.make_async_copy(own.at[level], own_f32.at[level], weight_sem.at[0, level]),
            pltpu.make_async_copy(partner.at[level], partner_f32.at[level], weight_sem.at[1, level]),
        )

    def exchange(level, c, back):
        slot = level - 1
        way = 4 * back + slot
        return pltpu.make_async_remote_copy(
            src_ref=(term if back else state).at[slot, c],
            dst_ref=(carried if back else other).at[slot, c],
            send_sem=send_sem.at[way, c],
            recv_sem=recv_sem.at[way, c],
            device_id=partners[level],
            device_id_type=MESH,
        )

    copy_in[0].start()
    for copy in weights_in(0):
        copy.start()

    barrier = pltpu.get_barrier_semaphore()
    for level in range(1, LEVELS):
        pl.semaphore_signal(barrier, inc=1, device_id=partners[level], device_id_type=MESH)
    pl.semaphore_signal(barrier, inc=1, device_id=neighbour, device_id_type=MESH)

    def prepare(level):
        for copy in weights_in(level):
            copy.wait()

        @pl.loop(0, 2)
        def _(b):
            for i, source in enumerate((own_f32, partner_f32)):
                for part in range(2):
                    high, low = split(source[level, b, part])
                    place = pl.ds((2 * i + part) * k, k)
                    w_high[level, b, place, :] = high
                    w_low[level, b, place, :] = low

    def forward(level, mine, theirs, b):
        (ur, ui), (vr, vi) = mine, theirs
        real = jnp.concatenate([ur, -ui, vr, -vi], axis=1)
        imag = jnp.concatenate([ui, ur, vi, vr], axis=1)
        high, low = split(jnp.concatenate([real, imag], axis=0))
        both = dot(jnp.concatenate([high, low], axis=0), w_high[level, b])
        out = both[: 2 * size] + both[2 * size :] + dot(high, w_low[level, b])
        return out[:size], out[size:]

    def adjoint_side(gr, gi):
        first = jnp.concatenate([gr, gi], axis=0)
        second = jnp.concatenate([gi, -gr], axis=0)
        return split(jnp.concatenate([first, second], axis=1))

    def adjoint(level, which, side, b):
        high, low = side

        def weight(w):
            return jnp.concatenate(
                [w[level, b, pl.ds((2 * which + part) * k, k), :] for part in range(2)], axis=1
            )

        both = dot_t(jnp.concatenate([high, low], axis=0), weight(w_high))
        out = both[: 2 * size] + both[2 * size :] + dot_t(high, weight(w_low))
        return out[:size], out[size:]

    def put(ref, index, value):
        for part in range(2):
            ref[(*index, part)] = value[part]

    def back_level(level, c, grads):
        sides = [adjoint_side(*g) for g in grads]
        for b in range(2):
            put(term, (level - 1, c, b), adjoint(level, 1, sides[b], b))
        exchange(level, c, 1).start()
        for b in range(2):
            put(kept, (level - 1, c, b), adjoint(level, 0, sides[b], b))

    def arrived(level, c):
        exchange(level, c, 1).wait_recv()
        return [
            [kept[level - 1, c, b, part] + carried[level - 1, c, b, part] for part in range(2)]
            for b in range(2)
        ]

    def first(c):
        at = pl.ds(pl.multiple_of(c * size, size), size)
        boxes = [[start[b, part, at, :] for part in range(2)] for b in range(2)]
        for b in range(2):
            put(state, (0, c, b), forward(0, boxes[b], boxes[1 - b], b))

        @pl.when(c == 0)
        def _():
            pl.semaphore_wait(barrier, LEVELS)

        exchange(1, c, 0).start()

    def middle(level, c):
        @pl.when(c == 0)
        def _():
            prepare(level)

        exchange(level, c, 0).wait_recv()
        if level == 2:
            pl.semaphore_signal(pace_sem, inc=1, device_id=neighbour, device_id_type=MESH)
        slot = level - 1
        for b in range(2):
            mine, theirs = ([ref[slot, c, b, part] for part in range(2)] for ref in (state, other))
            put(state, (slot + 1, c, b), forward(level, mine, theirs, b))
        if level == 1:
            @pl.when(c >= AHEAD)
            def _():
                pl.semaphore_wait(pace_sem, 1)

        exchange(level + 1, c, 0).start()

    def turn(c):
        @pl.when(c == 0)
        def _():
            prepare(4)
            copy_in[1].wait()

        exchange(4, c, 0).wait_recv()
        at = pl.ds(pl.multiple_of(c * size, size), size)
        grads = []
        for b in range(2):
            mine, theirs = ([ref[3, c, b, part] for part in range(2)] for ref in (state, other))
            out = forward(4, mine, theirs, b)
            grads.append([out[part] - data[b, part, at, :] for part in range(2)])
            for part in range(2):
                residual[b, part, at, :] = grads[b][part]
        back_level(4, c, grads)

    def last(c):
        for back in range(2):
            for level in range(1, LEVELS):
                exchange(level, c, back).wait_send()
        sides = [adjoint_side(*g) for g in arrived(1, c)]
        at = pl.ds(pl.multiple_of(c * size, size), size)
        for b in range(2):
            mine = adjoint(0, 0, sides[b], b)
            theirs = adjoint(0, 1, sides[1 - b], 1 - b)
            for part in range(2):
                gradient[b, part, at, :] = mine[part] + theirs[part]

    tasks = [
        first,
        functools.partial(middle, 1),
        functools.partial(middle, 2),
        functools.partial(middle, 3),
        turn,
        lambda c: back_level(3, c, arrived(4, c)),
        lambda c: back_level(2, c, arrived(3, c)),
        lambda c: back_level(1, c, arrived(2, c)),
        last,
    ]

    copy_in[0].wait()
    prepare(0)
    for level in range(1, LEVELS):
        for copy in weights_in(level):
            copy.start()
    copy_in[1].start()

    @pl.loop(0, chunks + DELAYS[-1])
    def _(step):
        for task, delay in zip(tasks, DELAYS):
            c = step - delay
            pl.when(jnp.logical_and(c >= 0, c < chunks))(functools.partial(task, c))

    pl.semaphore_wait(pace_sem, min(AHEAD, chunks))


def write_back(residual, gradient, residual_out, gradient_out, sem):
    copies = [
        pltpu.make_async_copy(source, target, sem.at[i])
        for i, (source, target) in enumerate(((residual, residual_out), (gradient, gradient_out)))
    ]
    for copy in copies:
        copy.start()
    for copy in copies:
        copy.wait()


def shards(model, observed, own, partner):
    boxes, parts, rows, k = model.shape
    size = rows // CHUNKS
    chunked = (CHUNKS, boxes, parts, size, k)
    whole = pltpu.VMEM((LEVELS - 1, *chunked), F32)
    flops = 2 * 2 * LEVELS * boxes * 8 * rows * k * k * 3
    results = pl.pallas_call(
        kernel,
        out_shape=[jax.ShapeDtypeStruct(model.shape, F32)] * 2,
        in_specs=[pl.BlockSpec(memory_space=pltpu.HBM)] * 4,
        out_specs=[pl.BlockSpec(memory_space=pltpu.VMEM)] * 2,
        scratch_shapes=[
            pltpu.VMEM(model.shape, F32),
            pltpu.VMEM(model.shape, F32),
            pltpu.VMEM(own.shape, F32),
            pltpu.VMEM(own.shape, F32),
            pltpu.VMEM((LEVELS, boxes, 4 * k, k), BF16),
            pltpu.VMEM((LEVELS, boxes, 4 * k, k), BF16),
            whole, whole, whole, whole, whole,
            pltpu.SemaphoreType.DMA((2,)),
            pltpu.SemaphoreType.DMA((2, LEVELS)),
            pltpu.SemaphoreType.DMA((8, CHUNKS)),
            pltpu.SemaphoreType.DMA((8, CHUNKS)),
            pltpu.SemaphoreType.REGULAR,
        ],
        compiler_params=pltpu.CompilerParams(
            collective_id=0, has_side_effects=True, vmem_limit_bytes=51 * 2**20
        ),
        cost_estimate=pl.CostEstimate(flops=flops, bytes_accessed=14 * 2**20, transcendentals=0),
    )(model, observed, own, partner)
    return pl.pallas_call(
        write_back,
        out_shape=[jax.ShapeDtypeStruct(model.shape, F32)] * 2,
        in_specs=[pl.BlockSpec(memory_space=pl.ANY)] * 2,
        out_specs=[pl.BlockSpec(memory_space=pltpu.HBM)] * 2,
        scratch_shapes=[pltpu.SemaphoreType.DMA((2,))],
        compiler_params=pltpu.CompilerParams(vmem_limit_bytes=2**20),
        cost_estimate=pl.CostEstimate(flops=0, bytes_accessed=4 * 2**20, transcendentals=0),
    )(*results)


def solution(mesh):
    boxes = P(("wide", "narrow"), None, None, None)
    weights = P(None, ("wide", "narrow"), None, None, None)
    return jax.shard_map(
        shards,
        mesh=mesh,
        in_specs=(boxes, boxes, weights, weights),
        out_specs=(boxes, boxes),
        check_vma=False,
    )
```
